32 devices in a mesh: chan: 8 (over z, x), kred: 4 (over y, core).
Axes of the slice: x: 2, y: 2, z: 4, core: 2. Of those that a mesh axis runs over, the one named last changes fastest.
Arguments:
- t2_ph: bfloat16 [8, 4096, 128], P('chan', 'kred'), may hold values from -6 to 6
- dest_owner: int32 [8, 4096], P('chan', 'kred'), may hold values from 0 to 7, as said below
- source_owner: int32 [8, 4096], P('chan', 'kred'), may hold values from 0 to 7, as said below
- source_slot: int32 [8, 4096], P('chan', 'kred'), may hold values from 0 to 255
- hole_count: int32 [8], P('chan'), may hold values from 32 to 128
- ladder_v: bfloat16 [8, 4096, 4096], P('chan', None, 'kred'), as said below
Outputs:
- ladder_out: bfloat16 [8, 4096, 128], P('chan', 'kred')
The draws below stay inside these ranges and needn't reach their ends.
Inputs may be any that keep to these rules, and one draw needn't show every extreme that they name: Within each aligned block of 1024 rows of dest_owner[s] at most 256 rows name the same channel, and some channel is named by exactly 256; every channel is named by exactly 1024 rows of the same block index over all s. The pairs (source_owner, source_slot) of one channel and one aligned block of 1024 columns are distinct and name exactly the rows that dest_owner sends to that channel from that block. `ladder_v`: symmetric in its last two dimensions for each channel.
All inputs are finite; a program needn't handle non-finite values.
Results may differ from the reference program's by a relative error of at most 0.001.
Values may be sent and summed in bfloat16 or wider, within the bound.
A program may use at most 64 MiB of HBM per device.

```python
import jax
import jax.numpy as jnp
from jax import lax

P_SIZE = 4096
H = 128
SLAB = 1024
RECV_CAP = 256
N_CHAN = 8
N_KRED = 4


def recouple_lists(key):
    seeded = jax.random.fold_in(key, 7)
    keys = jax.random.split(seeded, 4)
    base_rows = SLAB // N_CHAN
    extra_rows = SLAB % N_CHAN
    channels = jnp.arange(N_CHAN, dtype=jnp.int32)
    base_weights = base_rows + (channels >= N_CHAN - extra_rows).astype(jnp.int32)
    busiest_offset = 0 if RECV_CAP == 2 * base_rows else N_CHAN - 1
    emptied_offset = 1 if busiest_offset == 0 else 0
    base_weights = base_weights + base_rows * (channels == busiest_offset).astype(jnp.int32) - base_rows * (channels == emptied_offset).astype(jnp.int32)
    shifts = jax.random.randint(keys[0], (N_KRED,), 0, N_CHAN)
    weights = base_weights[(channels[None, :] + shifts[:, None]) % N_CHAN]
    offsets = (channels[None, :] - channels[:, None]) % N_CHAN
    counts = weights[:, offsets]
    positions = jnp.arange(SLAB, dtype=jnp.int32)
    cumulative = jnp.cumsum(counts, axis=2)
    sorted_dest = jnp.sum((cumulative[:, :, None, :] <= positions[None, None, :, None]).astype(jnp.int32), axis=3)
    send_keys = jax.random.split(keys[2], N_KRED * N_CHAN)
    send_perms = jax.vmap(lambda kk: jax.random.permutation(kk, SLAB).astype(jnp.int32))(send_keys).reshape(N_KRED, N_CHAN, SLAB)
    dest = jnp.take_along_axis(sorted_dest, send_perms, axis=2)
    dest_owner = jnp.transpose(dest, (1, 0, 2)).reshape(N_CHAN, N_KRED * SLAB)
    incoming = jnp.transpose(counts, (0, 2, 1))
    cum_in = jnp.cumsum(incoming, axis=2)
    src_sorted = jnp.sum((cum_in[:, :, None, :] <= positions[None, None, :, None]).astype(jnp.int32), axis=3)
    starts = jnp.take_along_axis(cum_in - incoming, src_sorted, axis=2)
    slot_sorted = positions[None, None, :] - starts
    recv_keys = jax.random.split(keys[3], N_KRED * N_CHAN)
    recv_perms = jax.vmap(lambda kk: jax.random.permutation(kk, SLAB).astype(jnp.int32))(recv_keys).reshape(N_KRED, N_CHAN, SLAB)
    inverse = jnp.argsort(recv_perms, axis=2).astype(jnp.int32)
    src_owner = jnp.take_along_axis(src_sorted, inverse, axis=2)
    src_slot = jnp.take_along_axis(slot_sorted, inverse, axis=2)
    src_owner = jnp.transpose(src_owner, (1, 0, 2)).reshape(N_CHAN, N_KRED * SLAB)
    src_slot = jnp.transpose(src_slot, (1, 0, 2)).reshape(N_CHAN, N_KRED * SLAB)
    return (dest_owner.astype(jnp.int32), src_owner.astype(jnp.int32), src_slot.astype(jnp.int32))


def draw_dest_owner(key, part):
    return recouple_lists(key)[0]


def draw_source_owner(key, part):
    return recouple_lists(key)[1]


def draw_source_slot(key, part):
    return recouple_lists(key)[2]


def draw_hole_count(key, part):
    seeded = jax.random.fold_in(key, 11)
    first, second = jax.random.split(seeded)
    counts = jax.random.randint(first, (N_CHAN,), H // 4, H + 1).astype(jnp.int32)
    fullest = jax.random.randint(second, (), 0, N_CHAN)
    return counts.at[fullest].set(H)


def draw_ladder_v(key, part):
    seeded = jax.random.fold_in(key, 13)
    raw = jax.random.normal(seeded, (N_CHAN, P_SIZE, P_SIZE), jnp.float32)
    symmetric = (raw + jnp.swapaxes(raw, 1, 2)) * (1.0 / (2.0 * P_SIZE) ** 0.5)
    return symmetric.astype(jnp.bfloat16)


def shard_levels(key, dims, pieces, low, high):
    gain, own = 1.0, jax.random.fold_in(key, 6)
    for axis_at, parts in pieces:
        steps = jnp.exp(jax.random.uniform(jax.random.fold_in(own, axis_at), (parts,), jnp.float32, low / len(pieces), high / len(pieces)))
        gain = gain * jnp.repeat(steps, dims[axis_at] // parts).reshape([-1 if axis == axis_at else 1 for axis in range(len(dims))])
    return gain


def normal_values(stream_key, extent, width, reach, cuts=(), held_as=jnp.bfloat16):
    drawn = width * jax.random.normal(stream_key, extent, jnp.float32)
    if cuts:
        drawn = drawn * shard_levels(stream_key, extent, cuts, -0.22, 0.18)
    return jnp.clip(drawn, -reach, reach).astype(held_as)


def setup_inputs(seed: int = 0) -> dict:
    arg_keys = jax.random.split(jax.random.key(seed), 7)
    return {
        "t2_ph": normal_values(arg_keys[0], (N_CHAN, P_SIZE, H), 1.0, 6.0, ((0, 8), (1, 4))),
        "dest_owner": draw_dest_owner(jax.random.fold_in(arg_keys[6], 71), 0),
        "source_owner": draw_source_owner(jax.random.fold_in(arg_keys[6], 71), 0),
        "source_slot": draw_source_slot(jax.random.fold_in(arg_keys[6], 71), 0),
        "hole_count": draw_hole_count(jax.random.fold_in(arg_keys[6], 71), 0),
        "ladder_v": draw_ladder_v(jax.random.fold_in(arg_keys[6], 71), 0),
    }


def reference(t2_ph, dest_owner, source_owner, source_slot, hole_count, ladder_v):
    owners = dest_owner.reshape(N_CHAN, N_KRED, SLAB)
    channels = jnp.arange(N_CHAN, dtype=jnp.int32)
    matches = (owners[..., None] == channels[None, None, None, :]).astype(jnp.int32)
    before = jnp.sum((jnp.cumsum(matches, axis=2) - matches) * matches, axis=3)
    target = owners * RECV_CAP + before
    row_ids = jnp.broadcast_to(jnp.arange(SLAB, dtype=jnp.int32)[None, None, :], owners.shape)
    sender_ids = jnp.broadcast_to(channels[:, None, None], owners.shape)
    lane_ids = jnp.broadcast_to(jnp.arange(N_KRED, dtype=jnp.int32)[None, :, None], owners.shape)
    table = jnp.zeros((N_CHAN, N_KRED, N_CHAN * RECV_CAP), jnp.int32)
    table = table.at[sender_ids, lane_ids, target].set(row_ids)
    senders = source_owner.reshape(N_CHAN, N_KRED, SLAB)
    slots = source_slot.reshape(N_CHAN, N_KRED, SLAB)
    receivers = sender_ids
    chosen = table[senders, lane_ids, receivers * RECV_CAP + slots]
    recoupled = t2_ph[senders, lane_ids * SLAB + chosen].reshape(N_CHAN, P_SIZE, H)

    def one_channel(operands):
        interaction, amplitudes = operands
        return jnp.dot(interaction, amplitudes, preferred_element_type=jnp.float32)

    ladder = lax.map(one_channel, (ladder_v, recoupled))
    columns = jnp.arange(H, dtype=jnp.int32)
    masked = jnp.where(columns[None, None, :] < hole_count[:, None, None], ladder, jnp.float32(0.0))
    return masked.astype(jnp.bfloat16)
```

```python
import functools

import jax
import jax.numpy as jnp
from jax import lax
from jax.experimental import pallas as pl
from jax.experimental.pallas import tpu as pltpu
from jax.sharding import PartitionSpec as P

MESH = pl.DeviceIdType.MESH
F32 = jnp.float32
BF16 = jnp.bfloat16


def one_hot(count, row):
    lanes = row.shape[1]
    index = lax.broadcasted_iota(jnp.int32, (count, lanes), 0)
    if count <= 256:
        hit = index.astype(F32).astype(BF16) == row.astype(F32).astype(BF16)
    else:
        hit = index == row
    return jnp.where(hit, jnp.ones((), BF16), jnp.zeros((), BF16))


def row_numbers(owners, n_chan):
    rows = owners.shape[1]
    blocks = rows // 128
    channel = lax.broadcasted_iota(jnp.int32, (n_chan, 128), 0)
    hits = [
        (owners[:, b * 128 : (b + 1) * 128] == channel).astype(F32) for b in range(blocks)
    ]
    above = lax.broadcasted_iota(jnp.int32, (128, 128), 0) < lax.broadcasted_iota(
        jnp.int32, (128, 128), 1
    )
    inside = jnp.dot(
        jnp.concatenate(hits, axis=0).astype(BF16),
        jnp.where(above, 1.0, 0.0).astype(BF16),
        preferred_element_type=F32,
    )
    numbers = []
    offset = jnp.zeros((n_chan, 1), F32)
    for b in range(blocks):
        here = inside[b * n_chan : (b + 1) * n_chan] + offset
        numbers.append(jnp.sum(here * hits[b], axis=0, keepdims=True))
        offset = offset + jnp.sum(hits[b], axis=1, keepdims=True)
    return jnp.concatenate(numbers, axis=1).astype(jnp.int32)


def kernel(
    n_chan,
    n_kred,
    t2_ref,
    dest_ref,
    owner_ref,
    slot_ref,
    hole_ref,
    v_hbm,
    out_ref,
    outbox,
    arrived,
    picks,
    slabs,
    v_ref,
    acc,
    part,
    v_sem,
    a_send,
    a_recv,
    y_send,
    y_recv,
    s_send,
    s_recv,
    f_send,
    f_recv,
):
    chan = lax.axis_index("chan")
    kred = lax.axis_index("kred")
    n_outer = n_kred // 2
    inner = kred % 2
    outer = kred // 2
    sibling = {"kred": outer * 2 + (1 - inner)}
    capacity = outbox.shape[1]
    slab = t2_ref.shape[1]
    pieces, wide = slabs.shape[1], slabs.shape[3]

    barrier = pltpu.get_barrier_semaphore()
    for o in range(1, n_chan):
        pl.semaphore_signal(
            barrier, inc=1, device_id={"chan": (chan + o) % n_chan}, device_id_type=MESH
        )
    pl.semaphore_signal(barrier, inc=1, device_id=sibling, device_id_type=MESH)
    for d in range(1, n_outer):
        pl.semaphore_signal(
            barrier,
            inc=1,
            device_id={"kred": ((outer + d) % n_outer) * 2 + inner},
            device_id_type=MESH,
        )

    load_v = pltpu.make_async_copy(v_hbm.at[0], v_ref, v_sem)
    load_v.start()

    owners = dest_ref[...]
    numbers = row_numbers(owners, n_chan)
    order = sorted(range(1, n_chan), key=lambda o: abs(2 * o - n_chan))
    rows = t2_ref[0]

    def packed(channel):
        choose = one_hot(capacity, jnp.where(owners == channel, numbers, -1))
        return jnp.dot(choose, rows, preferred_element_type=F32).astype(BF16)

    sends = {}
    for at, o in enumerate(order):
        partner = (chan + o) % n_chan
        outbox[o] = packed(partner)
        if at == 0:
            pl.semaphore_wait(barrier, n_chan - 1 + 1 + n_outer - 1)
        sends[o] = pltpu.make_async_remote_copy(
            src_ref=outbox.at[o],
            dst_ref=arrived.at[o],
            send_sem=a_send.at[o],
            recv_sem=a_recv.at[o],
            device_id={"chan": partner},
            device_id_type=MESH,
        )
        sends[o].start()
    own = packed(chan)

    source = owner_ref[...]
    slots = slot_ref[...]
    for o in range(n_chan):
        sender = (chan - o + n_chan) % n_chan
        picks[o] = one_hot(capacity, jnp.where(source == sender, slots, -1))

    def spread(block, o, cols):
        return lax.dot_general(
            block, picks[o, :, cols], (((0,), (0,)), ((), ())), preferred_element_type=F32
        )

    last = order[-1]
    part[...] = spread(own, 0, slice(0, slab))
    for o in order[:-1]:
        sends[o].wait_recv()
        part[...] += spread(arrived[o], o, slice(0, slab))
    if order:
        sends[last].wait_recv()
    across, beside = {}, {}
    for i in range(pieces):
        cols = slice(i * wide, (i + 1) * wide)
        piece = part[:, cols] + spread(arrived[last], last, cols)
        slabs[0, i] = piece.astype(BF16)
        for d in range(1, n_outer):
            across[d, i] = pltpu.make_async_remote_copy(
                src_ref=slabs.at[0, i],
                dst_ref=slabs.at[2 * d, i],
                send_sem=y_send.at[d, i],
                recv_sem=y_recv.at[d, i],
                device_id={"kred": ((outer + d) % n_outer) * 2 + inner},
                device_id_type=MESH,
            )
            across[d, i].start()
        beside[i] = pltpu.make_async_remote_copy(
            src_ref=slabs.at[0, i],
            dst_ref=slabs.at[1, i],
            send_sem=s_send.at[i],
            recv_sem=s_recv.at[i],
            device_id=sibling,
            device_id_type=MESH,
        )
        beside[i].start()

    def product(place, i, index):
        start = pl.multiple_of(index * slab + i * wide, wide)
        return jnp.dot(
            slabs[place, i], v_ref[pl.ds(start, wide), :], preferred_element_type=F32
        )

    load_v.wait()
    acc[...] = product(0, 0, kred)
    for i in range(1, pieces):
        acc[...] += product(0, i, kred)
    for i in range(pieces):
        beside[i].wait_recv()
        acc[...] += product(1, i, outer * 2 + (1 - inner))
    onward = {}
    for d in range(1, n_outer):
        from_outer = (outer - d + n_outer) % n_outer
        for i in range(pieces):
            across[d, i].wait_recv()
            onward[d, i] = pltpu.make_async_remote_copy(
                src_ref=slabs.at[2 * d, i],
                dst_ref=slabs.at[2 * d + 1, i],
                send_sem=f_send.at[d, i],
                recv_sem=f_recv.at[d, i],
                device_id=sibling,
                device_id_type=MESH,
            )
            onward[d, i].start()
            acc[...] += product(2 * d, i, from_outer * 2 + inner)
            onward[d, i].wait_recv()
            acc[...] += product(2 * d + 1, i, from_outer * 2 + (1 - inner))

    live = lax.broadcasted_iota(jnp.int32, (1, acc.shape[0]), 1) < hole_ref[0]
    out_ref[0] = jnp.where(live, acc[...].T, 0.0).astype(BF16)

    for copies in (sends, across, beside, onward):
        for copy in copies.values():
            copy.wait_send()


def on_device(n_chan, n_kred, t2_ph, dest_owner, source_owner, source_slot, hole_count, ladder_v):
    slab, width = t2_ph.shape[1:]
    capacity = 2 * slab // n_chan
    capacity = -(-capacity // 16) * 16
    total = ladder_v.shape[1]
    wide = 256 if slab % 256 == 0 else slab
    pieces = slab // wide
    n_outer = n_kred // 2
    vmem = pl.BlockSpec(memory_space=pltpu.VMEM)
    dma = pltpu.SemaphoreType.DMA
    return pl.pallas_call(
        functools.partial(kernel, n_chan, n_kred),
        out_shape=jax.ShapeDtypeStruct((1, slab, width), BF16),
        in_specs=[
            vmem,
            vmem,
            vmem,
            vmem,
            pl.BlockSpec(memory_space=pltpu.SMEM),
            pl.BlockSpec(memory_space=pl.ANY),
        ],
        out_specs=vmem,
        scratch_shapes=[
            pltpu.VMEM((n_chan, capacity, width), BF16),
            pltpu.VMEM((n_chan, capacity, width), BF16),
            pltpu.VMEM((n_chan, capacity, slab), BF16),
            pltpu.VMEM((n_kred, pieces, width, wide), BF16),
            pltpu.VMEM((total, slab), BF16),
            pltpu.VMEM((width, slab), F32),
            pltpu.VMEM((width, slab), F32),
            dma,
            dma((n_chan,)),
            dma((n_chan,)),
            dma((n_outer, pieces)),
            dma((n_outer, pieces)),
            dma((pieces,)),
            dma((pieces,)),
            dma((n_outer, pieces)),
            dma((n_outer, pieces)),
        ],
        compiler_params=pltpu.CompilerParams(
            collective_id=0, has_side_effects=True, vmem_limit_bytes=56 * 2**20
        ),
        cost_estimate=pl.CostEstimate(
            flops=2 * total * slab * width, bytes_accessed=2 * total * slab, transcendentals=0
        ),
    )(t2_ph, dest_owner, source_owner, source_slot, hole_count, ladder_v)


def solution(mesh):
    placed = (
        P("chan", "kred", None),
        P("chan", "kred"),
        P("chan", "kred"),
        P("chan", "kred"),
        P("chan"),
        P("chan", None, "kred"),
    )
    return jax.shard_map(
        functools.partial(on_device, mesh.shape["chan"], mesh.shape["kred"]),
        mesh=mesh,
        in_specs=placed,
        out_specs=P("chan", "kred", None),
        check_vma=False,
    )
```

```python
import functools

import jax
import jax.numpy as jnp
from jax import lax
from jax.experimental import pallas as pl
from jax.experimental.pallas import tpu as pltpu
from jax.sharding import PartitionSpec as P

MESH = pl.DeviceIdType.MESH
F32 = jnp.float32
BF16 = jnp.bfloat16


def one_hot(count, row):
    lanes = row.shape[1]
    index = lax.broadcasted_iota(jnp.int32, (count, lanes), 0)
    if count <= 256:
        hit = index.astype(F32).astype(BF16) == row.astype(F32).astype(BF16)
    else:
        hit = index == row
    return jnp.where(hit, jnp.ones((), BF16), jnp.zeros((), BF16))


def row_numbers(owners, n_chan):
    rows = owners.shape[1]
    blocks = rows // 128
    channel = lax.broadcasted_iota(jnp.int32, (n_chan, 128), 0)
    hits = [
        (owners[:, b * 128 : (b + 1) * 128] == channel).astype(F32) for b in range(blocks)
    ]
    above = lax.broadcasted_iota(jnp.int32, (128, 128), 0) < lax.broadcasted_iota(
        jnp.int32, (128, 128), 1
    )
    inside = jnp.dot(
        jnp.concatenate(hits, axis=0).astype(BF16),
        jnp.where(above, 1.0, 0.0).astype(BF16),
        preferred_element_type=F32,
    )
    numbers = []
    offset = jnp.zeros((n_chan, 1), F32)
    for b in range(blocks):
        here = inside[b * n_chan : (b + 1) * n_chan] + offset
        numbers.append(jnp.sum(here * hits[b], axis=0, keepdims=True))
        offset = offset + jnp.sum(hits[b], axis=1, keepdims=True)
    return jnp.concatenate(numbers, axis=1).astype(jnp.int32)


def partners(me, n_chan):
    if n_chan & (n_chan - 1) == 0:

        def flipped(step):
            index, bit = 0, 1
            while bit < n_chan:
                index = index + ((me // bit + step // bit) % 2) * bit
                bit *= 2
            return index

        far = list(range(n_chan // 2, n_chan))
        near = list(range(1, n_chan // 2))
        order = []
        while far or near:
            order += far[:2] if not order else far[:1]
            far = far[2:] if len(order) == 2 else far[1:]
            order += near[:1]
            near = near[1:]
        return flipped, flipped, order
    return (
        lambda step: (me + step) % n_chan,
        lambda step: (me - step + n_chan) % n_chan,
        list(range(1, n_chan)),
    )


def kernel(
    n_chan,
    n_kred,
    t2_hbm,
    dest_hbm,
    owner_hbm,
    slot_hbm,
    hole_hbm,
    v_hbm,
    out_ref,
    t2_ref,
    dest_ref,
    lists,
    hole_ref,
    outbox,
    arrived,
    passed,
    picks,
    slabs,
    v_ref,
    acc,
    part,
    in_sem,
    v_sem,
    a_send,
    a_recv,
    p_send,
    p_recv,
    l_send,
    l_recv,
    s_send,
    s_recv,
):
    chan = lax.axis_index("chan")
    kred = lax.axis_index("kred")
    n_outer = n_kred // 2
    inner = kred % 2
    outer = kred // 2
    sibling = {"kred": outer * 2 + (1 - inner)}
    capacity = outbox.shape[1]
    slab = t2_ref.shape[0]
    pieces, wide = slabs.shape[1], slabs.shape[3]
    receiver, sender, order = partners(chan, n_chan)

    def beyond(d):
        return {"kred": ((outer + d) % n_outer) * 2 + inner}

    load_dest = pltpu.make_async_copy(dest_hbm, dest_ref, in_sem.at[0])
    load_t2 = pltpu.make_async_copy(t2_hbm.at[0], t2_ref, in_sem.at[1])
    load_owner = pltpu.make_async_copy(owner_hbm, lists.at[0, 0], in_sem.at[2])
    load_slot = pltpu.make_async_copy(slot_hbm, lists.at[0, 1], in_sem.at[3])
    load_hole = pltpu.make_async_copy(hole_hbm, hole_ref, in_sem.at[4])
    load_v = pltpu.make_async_copy(v_hbm.at[0], v_ref, v_sem)
    load_dest.start()
    load_t2.start()
    load_owner.start()
    load_slot.start()
    load_hole.start()

    barrier = pltpu.get_barrier_semaphore()
    for o in order:
        pl.semaphore_signal(
            barrier, inc=1, device_id={"chan": receiver(o)}, device_id_type=MESH
        )
    pl.semaphore_signal(barrier, inc=1, device_id=sibling, device_id_type=MESH)
    for d in range(1, n_outer):
        pl.semaphore_signal(barrier, inc=1, device_id=beyond(d), device_id_type=MESH)

    load_dest.wait()
    owners = dest_ref[...]
    numbers = row_numbers(owners, n_chan)
    load_t2.wait()
    rows = t2_ref[...]

    def packed(channel):
        choose = one_hot(capacity, jnp.where(owners == channel, numbers, -1))
        return jnp.dot(choose, rows, preferred_element_type=F32).astype(BF16)

    sends, passes, listed = {}, {}, {}
    for at, o in enumerate(order):
        outbox[o] = packed(receiver(o))
        if at == 0:
            pl.semaphore_wait(barrier, n_chan - 1 + 1 + n_outer - 1)
        sends[o] = pltpu.make_async_remote_copy(
            src_ref=outbox.at[o],
            dst_ref=arrived.at[o],
            send_sem=a_send.at[o],
            recv_sem=a_recv.at[o],
            device_id={"chan": receiver(o)},
            device_id_type=MESH,
        )
        sends[o].start()
    load_v.start()
    arrived[0] = packed(chan)

    def pass_on(o):
        for d in range(1, n_outer):
            passes[d, o] = pltpu.make_async_remote_copy(
                src_ref=arrived.at[o],
                dst_ref=passed.at[d, o],
                send_sem=p_send.at[d, o],
                recv_sem=p_recv.at[d, o],
                device_id=beyond(d),
                device_id_type=MESH,
            )
            passes[d, o].start()

    load_owner.wait()
    load_slot.wait()
    for d in range(1, n_outer):
        listed[d] = pltpu.make_async_remote_copy(
            src_ref=lists.at[0],
            dst_ref=lists.at[d],
            send_sem=l_send.at[d],
            recv_sem=l_recv.at[d],
            device_id=beyond(d),
            device_id_type=MESH,
        )
        listed[d].start()
    pass_on(0)

    def lay_out(d):
        for o in [0] + order:
            mine = jnp.where(lists[d, 0] == sender(o), lists[d, 1], -1)
            picks[d, o] = one_hot(capacity, mine)

    def spread(d, o):
        block = arrived[o] if d == 0 else passed[d, o]
        term = lax.dot_general(
            block, picks[d, o], (((0,), (0,)), ((), ())), preferred_element_type=F32
        )
        if o == 0:
            part[d] = term
        else:
            part[d] += term

    shares = {}

    def finish(d):
        for i in range(pieces):
            slabs[2 * d, i] = part[d, :, i * wide : (i + 1) * wide].astype(BF16)
            shares[d, i] = pltpu.make_async_remote_copy(
                src_ref=slabs.at[2 * d, i],
                dst_ref=slabs.at[2 * d + 1, i],
                send_sem=s_send.at[d, i],
                recv_sem=s_recv.at[d, i],
                device_id=sibling,
                device_id_type=MESH,
            )
            shares[d, i].start()

    def product(d, i, theirs):
        index = ((outer - d + n_outer) % n_outer) * 2
        index = index + (1 - inner if theirs else inner)
        start = pl.multiple_of(index * slab + i * wide, wide)
        return jnp.dot(
            slabs[2 * d + theirs, i], v_ref[pl.ds(start, wide), :], preferred_element_type=F32
        )

    lay_out(0)
    for d in range(1, n_outer):
        listed[d].wait_recv()
        lay_out(d)
    steps = [0] + order
    lag = 2
    for at, o in enumerate(steps):
        if o:
            sends[o].wait_recv()
            pass_on(o)
        spread(0, o)
        if lag <= at < len(steps) - 1:
            for d in range(1, n_outer):
                passes[d, steps[at - lag]].wait_recv()
                spread(d, steps[at - lag])
    finish(0)
    load_v.wait()
    for d in range(1, n_outer):
        for o in steps[max(len(steps) - 1 - lag, 0) : -1]:
            passes[d, o].wait_recv()
            spread(d, o)
    acc[...] = product(0, 0, 0)
    for i in range(1, pieces):
        acc[...] += product(0, i, 0)
    for d in range(1, n_outer):
        passes[d, steps[-1]].wait_recv()
        spread(d, steps[-1])
        finish(d)
    for i in range(pieces):
        shares[0, i].wait_recv()
        acc[...] += product(0, i, 1)
    for d in range(1, n_outer):
        for i in range(pieces):
            acc[...] += product(d, i, 0)
        for i in range(pieces):
            shares[d, i].wait_recv()
            acc[...] += product(d, i, 1)

    load_hole.wait()
    live = lax.broadcasted_iota(jnp.int32, (1, acc.shape[0]), 1) < hole_ref[0]
    out_ref[0] = jnp.where(live, acc[...].T, 0.0).astype(BF16)

    for copies in (sends, listed, passes, shares):
        for copy in copies.values():
            copy.wait_send()


def on_device(n_chan, n_kred, t2_ph, dest_owner, source_owner, source_slot, hole_count, ladder_v):
    slab, width = t2_ph.shape[1:]
    capacity = 2 * slab // n_chan
    capacity = -(-capacity // 16) * 16
    total = ladder_v.shape[1]
    wide = 256 if slab % 256 == 0 else slab
    pieces = slab // wide
    n_outer = n_kred // 2
    dma = pltpu.SemaphoreType.DMA
    return pl.pallas_call(
        functools.partial(kernel, n_chan, n_kred),
        out_shape=pltpu.VMEM((1, slab, width), BF16),
        in_specs=[pl.BlockSpec(memory_space=pltpu.HBM)] * 6,
        out_specs=pl.BlockSpec(memory_space=pltpu.VMEM),
        scratch_shapes=[
            pltpu.VMEM((slab, width), BF16),
            pltpu.VMEM((1, slab), jnp.int32),
            pltpu.VMEM((n_outer, 2, 1, slab), jnp.int32),
            pltpu.SMEM((1,), jnp.int32),
            pltpu.VMEM((n_chan, capacity, width), BF16),
            pltpu.VMEM((n_chan, capacity, width), BF16),
            pltpu.VMEM((n_outer, n_chan, capacity, width), BF16),
            pltpu.VMEM((n_outer, n_chan, capacity, slab), BF16),
            pltpu.VMEM((n_kred, pieces, width, wide), BF16),
            pltpu.VMEM((total, slab), BF16),
            pltpu.VMEM((width, slab), F32),
            pltpu.VMEM((n_outer, width, slab), F32),
            dma((5,)),
            dma,
            dma((n_chan,)),
            dma((n_chan,)),
            dma((n_outer, n_chan)),
            dma((n_outer, n_chan)),
            dma((n_outer,)),
            dma((n_outer,)),
            dma((n_outer, pieces)),
            dma((n_outer, pieces)),
        ],
        compiler_params=pltpu.CompilerParams(
            collective_id=0, has_side_effects=True, vmem_limit_bytes=56 * 2**20
        ),
        cost_estimate=pl.CostEstimate(
            flops=2 * total * slab * width, bytes_accessed=2 * total * slab, transcendentals=0
        ),
    )(t2_ph, dest_owner, source_owner, source_slot, hole_count, ladder_v)


def solution(mesh):
    placed = (
        P("chan", "kred", None),
        P("chan", "kred"),
        P("chan", "kred"),
        P("chan", "kred"),
        P("chan"),
        P("chan", None, "kred"),
    )
    return jax.shard_map(
        functools.partial(on_device, mesh.shape["chan"], mesh.shape["kred"]),
        mesh=mesh,
        in_specs=placed,
        out_specs=P("chan", "kred", None),
        check_vma=False,
    )
```

```python
import functools

import jax
import jax.numpy as jnp
from jax import lax
from jax.experimental import pallas as pl
from jax.experimental.pallas import tpu as pltpu
from jax.sharding import PartitionSpec as P

MESH = pl.DeviceIdType.MESH
F32 = jnp.float32
BF16 = jnp.bfloat16


def one_hot(count, row):
    lanes = row.shape[1]
    index = lax.broadcasted_iota(jnp.int32, (count, lanes), 0)
    if count <= 256:
        hit = index.astype(F32).astype(BF16) == row.astype(F32).astype(BF16)
    else:
        hit = index == row
    return jnp.where(hit, jnp.ones((), BF16), jnp.zeros((), BF16))


def row_numbers(owners, n_chan):
    rows = owners.shape[1]
    blocks = rows // 128
    channel = lax.broadcasted_iota(jnp.int32, (n_chan, 128), 0)
    hits = [
        (owners[:, b * 128 : (b + 1) * 128] == channel).astype(F32) for b in range(blocks)
    ]
    above = lax.broadcasted_iota(jnp.int32, (128, 128), 0) < lax.broadcasted_iota(
        jnp.int32, (128, 128), 1
    )
    inside = jnp.dot(
        jnp.concatenate(hits, axis=0).astype(BF16),
        jnp.where(above, 1.0, 0.0).astype(BF16),
        preferred_element_type=F32,
    )
    numbers = []
    offset = jnp.zeros((n_chan, 1), F32)
    for b in range(blocks):
        here = inside[b * n_chan : (b + 1) * n_chan] + offset
        numbers.append(jnp.sum(here * hits[b], axis=0, keepdims=True))
        offset = offset + jnp.sum(hits[b], axis=1, keepdims=True)
    return jnp.concatenate(numbers, axis=1).astype(jnp.int32)


def partners(me, n_chan):
    if n_chan & (n_chan - 1) == 0:

        def flipped(step):
            index, bit = 0, 1
            while bit < n_chan:
                index = index + ((me // bit + step // bit) % 2) * bit
                bit *= 2
            return index

        far = list(range(n_chan // 2, n_chan))
        near = list(range(1, n_chan // 2))
        return flipped, flipped, near, far
    return (
        lambda step: (me + step) % n_chan,
        lambda step: (me - step + n_chan) % n_chan,
        list(range(1, n_chan)),
        [],
    )


def kernel(
    n_chan,
    n_kred,
    t2_hbm,
    dest_hbm,
    owner_hbm,
    slot_hbm,
    hole_hbm,
    v_hbm,
    out_ref,
    t2_ref,
    dest_ref,
    lists,
    hole_ref,
    outbox,
    arrived,
    passed,
    picks,
    slabs,
    v_ref,
    acc,
    part,
    in_sem,
    v_sem,
    a_send,
    a_recv,
    p_send,
    p_recv,
    l_send,
    l_recv,
    s_send,
    s_recv,
):
    chan = lax.axis_index("chan")
    kred = lax.axis_index("kred")
    n_outer = n_kred // 2
    inner = kred % 2
    outer = kred // 2
    sibling = {"kred": outer * 2 + (1 - inner)}
    capacity = outbox.shape[1]
    slab = t2_ref.shape[0]
    pieces, wide = slabs.shape[1], slabs.shape[3]
    receiver, sender, near, far = partners(chan, n_chan)
    order = near + far

    def beyond(d):
        return {"kred": ((outer + d) % n_outer) * 2 + inner}

    load_dest = pltpu.make_async_copy(dest_hbm, dest_ref, in_sem.at[0])
    load_t2 = pltpu.make_async_copy(t2_hbm.at[0], t2_ref, in_sem.at[1])
    load_owner = pltpu.make_async_copy(owner_hbm, lists.at[0, 0], in_sem.at[2])
    load_slot = pltpu.make_async_copy(slot_hbm, lists.at[0, 1], in_sem.at[3])
    load_hole = pltpu.make_async_copy(hole_hbm, hole_ref, in_sem.at[4])
    load_v = pltpu.make_async_copy(v_hbm.at[0], v_ref, v_sem)
    load_dest.start()
    load_t2.start()
    load_owner.start()
    load_slot.start()
    load_hole.start()

    barrier = pltpu.get_barrier_semaphore()
    for o in order:
        pl.semaphore_signal(
            barrier, inc=1, device_id={"chan": receiver(o)}, device_id_type=MESH
        )
    pl.semaphore_signal(barrier, inc=1, device_id=sibling, device_id_type=MESH)
    for d in range(1, n_outer):
        pl.semaphore_signal(barrier, inc=1, device_id=beyond(d), device_id_type=MESH)

    load_dest.wait()
    owners = dest_ref[...]
    numbers = row_numbers(owners, n_chan)
    load_t2.wait()
    rows = t2_ref[...]

    def packed(channel):
        choose = one_hot(capacity, jnp.where(owners == channel, numbers, -1))
        return jnp.dot(choose, rows, preferred_element_type=F32).astype(BF16)

    sends, passes, listed = {}, {}, {}
    for at, o in enumerate(far[:1] + near + far[1:]):
        outbox[o] = packed(receiver(o))
        if at == 0:
            pl.semaphore_wait(barrier, n_chan - 1 + 1 + n_outer - 1)
        sends[o] = pltpu.make_async_remote_copy(
            src_ref=outbox.at[o],
            dst_ref=arrived.at[o],
            send_sem=a_send.at[o],
            recv_sem=a_recv.at[o],
            device_id={"chan": receiver(o)},
            device_id_type=MESH,
        )
        if o not in far[1:]:
            sends[o].start()
    load_v.start()
    arrived[0] = packed(chan)

    def pass_on(o):
        for d in range(1, n_outer):
            passes[d, o] = pltpu.make_async_remote_copy(
                src_ref=arrived.at[o],
                dst_ref=passed.at[d, o],
                send_sem=p_send.at[d, o],
                recv_sem=p_recv.at[d, o],
                device_id=beyond(d),
                device_id_type=MESH,
            )
            passes[d, o].start()

    load_owner.wait()
    load_slot.wait()
    for d in range(1, n_outer):
        listed[d] = pltpu.make_async_remote_copy(
            src_ref=lists.at[0],
            dst_ref=lists.at[d],
            send_sem=l_send.at[d],
            recv_sem=l_recv.at[d],
            device_id=beyond(d),
            device_id_type=MESH,
        )
        listed[d].start()
    pass_on(0)

    def lay_out(d):
        for o in [0] + order:
            mine = jnp.where(lists[d, 0] == sender(o), lists[d, 1], -1)
            picks[d, o] = one_hot(capacity, mine)

    def spread(d, o):
        block = arrived[o] if d == 0 else passed[d, o]
        term = lax.dot_general(
            block, picks[d, o], (((0,), (0,)), ((), ())), preferred_element_type=F32
        )
        if o == 0:
            part[d] = term
        else:
            part[d] += term

    shares = {}

    def finish(d):
        for i in range(pieces):
            slabs[2 * d, i] = part[d, :, i * wide : (i + 1) * wide].astype(BF16)
            shares[d, i] = pltpu.make_async_remote_copy(
                src_ref=slabs.at[2 * d, i],
                dst_ref=slabs.at[2 * d + 1, i],
                send_sem=s_send.at[d, i],
                recv_sem=s_recv.at[d, i],
                device_id=sibling,
                device_id_type=MESH,
            )
            shares[d, i].start()

    def product(d, i, theirs):
        index = ((outer - d + n_outer) % n_outer) * 2
        index = index + (1 - inner if theirs else inner)
        start = pl.multiple_of(index * slab + i * wide, wide)
        return jnp.dot(
            slabs[2 * d + theirs, i], v_ref[pl.ds(start, wide), :], preferred_element_type=F32
        )

    lay_out(0)
    for d in range(1, n_outer):
        listed[d].wait_recv()
        lay_out(d)
    steps = [0] + order
    lag = 2
    for at, o in enumerate(steps):
        if o:
            sends[o].wait_recv()
            pass_on(o)
        if o in far[:-1]:
            sends[o].wait_send()
            sends[o + 1].start()
        spread(0, o)
        if lag <= at < len(steps) - 1:
            for d in range(1, n_outer):
                passes[d, steps[at - lag]].wait_recv()
                spread(d, steps[at - lag])
    finish(0)
    load_v.wait()
    for d in range(1, n_outer):
        for o in steps[max(len(steps) - 1 - lag, 0) : -1]:
            passes[d, o].wait_recv()
            spread(d, o)
    acc[...] = product(0, 0, 0)
    for i in range(1, pieces):
        acc[...] += product(0, i, 0)
    for d in range(1, n_outer):
        passes[d, steps[-1]].wait_recv()
        spread(d, steps[-1])
        finish(d)
    for i in range(pieces):
        shares[0, i].wait_recv()
        acc[...] += product(0, i, 1)
    for d in range(1, n_outer):
        for i in range(pieces):
            acc[...] += product(d, i, 0)
        for i in range(pieces):
            shares[d, i].wait_recv()
            acc[...] += product(d, i, 1)

    load_hole.wait()
    live = lax.broadcasted_iota(jnp.int32, (1, acc.shape[0]), 1) < hole_ref[0]
    out_ref[0] = jnp.where(live, acc[...].T, 0.0).astype(BF16)

    for o in near + far[-1:]:
        sends[o].wait_send()
    for copies in (listed, passes, shares):
        for copy in copies.values():
            copy.wait_send()


def on_device(n_chan, n_kred, t2_ph, dest_owner, source_owner, source_slot, hole_count, ladder_v):
    slab, width = t2_ph.shape[1:]
    capacity = 2 * slab // n_chan
    capacity = -(-capacity // 16) * 16
    total = ladder_v.shape[1]
    wide = 256 if slab % 256 == 0 else slab
    pieces = slab // wide
    n_outer = n_kred // 2
    dma = pltpu.SemaphoreType.DMA
    return pl.pallas_call(
        functools.partial(kernel, n_chan, n_kred),
        out_shape=pltpu.VMEM((1, slab, width), BF16),
        in_specs=[pl.BlockSpec(memory_space=pltpu.HBM)] * 6,
        out_specs=pl.BlockSpec(memory_space=pltpu.VMEM),
        scratch_shapes=[
            pltpu.VMEM((slab, width), BF16),
            pltpu.VMEM((1, slab), jnp.int32),
            pltpu.VMEM((n_outer, 2, 1, slab), jnp.int32),
            pltpu.SMEM((1,), jnp.int32),
            pltpu.VMEM((n_chan, capacity, width), BF16),
            pltpu.VMEM((n_chan, capacity, width), BF16),
            pltpu.VMEM((n_outer, n_chan, capacity, width), BF16),
            pltpu.VMEM((n_outer, n_chan, capacity, slab), BF16),
            pltpu.VMEM((n_kred, pieces, width, wide), BF16),
            pltpu.VMEM((total, slab), BF16),
            pltpu.VMEM((width, slab), F32),
            pltpu.VMEM((n_outer, width, slab), F32),
            dma((5,)),
            dma,
            dma((n_chan,)),
            dma((n_chan,)),
            dma((n_outer, n_chan)),
            dma((n_outer, n_chan)),
            dma((n_outer,)),
            dma((n_outer,)),
            dma((n_outer, pieces)),
            dma((n_outer, pieces)),
        ],
        compiler_params=pltpu.CompilerParams(
            collective_id=0, has_side_effects=True, vmem_limit_bytes=56 * 2**20
        ),
        cost_estimate=pl.CostEstimate(
            flops=2 * total * slab * width, bytes_accessed=2 * total * slab, transcendentals=0
        ),
    )(t2_ph, dest_owner, source_owner, source_slot, hole_count, ladder_v)


def solution(mesh):
    placed = (
        P("chan", "kred", None),
        P("chan", "kred"),
        P("chan", "kred"),
        P("chan", "kred"),
        P("chan"),
        P("chan", None, "kred"),
    )
    return jax.shard_map(
        functools.partial(on_device, mesh.shape["chan"], mesh.shape["kred"]),
        mesh=mesh,
        in_specs=placed,
        out_specs=P("chan", "kred", None),
        check_vma=False,
    )
```

```python
import functools

import jax
import jax.numpy as jnp
from jax import lax
from jax.experimental import pallas as pl
from jax.experimental.pallas import tpu as pltpu
from jax.sharding import PartitionSpec as P

MESH = pl.DeviceIdType.MESH
F32 = jnp.float32
BF16 = jnp.bfloat16


def one_hot(count, row):
    lanes = row.shape[1]
    index = lax.broadcasted_iota(jnp.int32, (count, lanes), 0)
    if count <= 256:
        hit = index.astype(F32).astype(BF16) == row.astype(F32).astype(BF16)
    else:
        hit = index == row
    return jnp.where(hit, jnp.ones((), BF16), jnp.zeros((), BF16))


def row_numbers(owners, n_chan):
    rows = owners.shape[1]
    blocks = rows // 128
    channel = lax.broadcasted_iota(jnp.int32, (n_chan, 128), 0)
    hits = [
        (owners[:, b * 128 : (b + 1) * 128] == channel).astype(F32) for b in range(blocks)
    ]
    above = lax.broadcasted_iota(jnp.int32, (128, 128), 0) < lax.broadcasted_iota(
        jnp.int32, (128, 128), 1
    )
    inside = jnp.dot(
        jnp.concatenate(hits, axis=0).astype(BF16),
        jnp.where(above, 1.0, 0.0).astype(BF16),
        preferred_element_type=F32,
    )
    numbers = []
    offset = jnp.zeros((n_chan, 1), F32)
    for b in range(blocks):
        here = inside[b * n_chan : (b + 1) * n_chan] + offset
        numbers.append(jnp.sum(here * hits[b], axis=0, keepdims=True))
        offset = offset + jnp.sum(hits[b], axis=1, keepdims=True)
    return jnp.concatenate(numbers, axis=1).astype(jnp.int32)


def partners(me, n_chan):
    if n_chan & (n_chan - 1) == 0:

        def flipped(step):
            index, bit = 0, 1
            while bit < n_chan:
                index = index + ((me // bit + step // bit) % 2) * bit
                bit *= 2
            return index

        far = list(range(n_chan // 2, n_chan))
        near = list(range(1, n_chan // 2))
        return flipped, flipped, near, far
    return (
        lambda step: (me + step) % n_chan,
        lambda step: (me - step + n_chan) % n_chan,
        list(range(1, n_chan)),
        [],
    )


def kernel(
    n_chan,
    n_kred,
    t2_hbm,
    dest_hbm,
    owner_hbm,
    slot_hbm,
    hole_hbm,
    v_hbm,
    out_ref,
    t2_ref,
    dest_ref,
    lists,
    hole_ref,
    outbox,
    arrived,
    picks,
    slabs,
    v_ref,
    acc,
    part,
    in_sem,
    v_sem,
    a_send,
    a_recv,
    y_send,
    y_recv,
    s_send,
    s_recv,
    f_send,
    f_recv,
):
    chan = lax.axis_index("chan")
    kred = lax.axis_index("kred")
    n_outer = n_kred // 2
    inner = kred % 2
    outer = kred // 2
    sibling = {"kred": outer * 2 + (1 - inner)}
    parts, tall, capacity = outbox.shape[1:]
    slab = t2_ref.shape[0]
    pieces, wide = slabs.shape[2], slabs.shape[4]
    receiver, sender, near, far = partners(chan, n_chan)
    order = near + far

    def beyond(d):
        return {"kred": ((outer + d) % n_outer) * 2 + inner}

    load_dest = pltpu.make_async_copy(dest_hbm, dest_ref, in_sem.at[0])
    load_t2 = pltpu.make_async_copy(t2_hbm.at[0], t2_ref, in_sem.at[1])
    load_owner = pltpu.make_async_copy(owner_hbm, lists.at[0], in_sem.at[2])
    load_slot = pltpu.make_async_copy(slot_hbm, lists.at[1], in_sem.at[3])
    load_hole = pltpu.make_async_copy(hole_hbm, hole_ref, in_sem.at[4])
    load_v = pltpu.make_async_copy(v_hbm.at[0], v_ref, v_sem)
    load_dest.start()
    load_t2.start()
    load_owner.start()
    load_slot.start()
    load_hole.start()

    barrier = pltpu.get_barrier_semaphore()
    for o in order:
        pl.semaphore_signal(
            barrier, inc=1, device_id={"chan": receiver(o)}, device_id_type=MESH
        )
    pl.semaphore_signal(barrier, inc=1, device_id=sibling, device_id_type=MESH)
    for d in range(1, n_outer):
        pl.semaphore_signal(barrier, inc=1, device_id=beyond(d), device_id_type=MESH)

    load_dest.wait()
    owners = dest_ref[...]
    numbers = row_numbers(owners, n_chan)
    load_t2.wait()
    rows = t2_ref[...]

    def pack(target, o, channel):
        choose = one_hot(capacity, jnp.where(owners == channel, numbers, -1))
        block = jnp.dot(choose, rows, preferred_element_type=F32).T.astype(BF16)
        for j in range(parts):
            target[o, j] = block[j * tall : (j + 1) * tall]

    sends = {}
    for at, o in enumerate(far + near):
        pack(outbox, o, receiver(o))
        if at == 0:
            pl.semaphore_wait(barrier, n_chan - 1 + 1 + n_outer - 1)
        for j in range(parts):
            sends[j, o] = pltpu.make_async_remote_copy(
                src_ref=outbox.at[o, j],
                dst_ref=arrived.at[o, j],
                send_sem=a_send.at[j, o],
                recv_sem=a_recv.at[j, o],
                device_id={"chan": receiver(o)},
                device_id_type=MESH,
            )
        sends[0, o].start()
    load_v.start()
    pack(arrived, 0, chan)
    load_owner.wait()
    load_slot.wait()
    for o in [0] + order:
        picks[o] = one_hot(capacity, jnp.where(lists[0] == sender(o), lists[1], -1))

    def spread(j, o, cols):
        return jnp.dot(arrived[o, j], picks[o, :, cols], preferred_element_type=F32)

    across, beside, onward = {}, {}, {}

    def gather(j):
        everything = slice(0, slab)
        part[...] = spread(j, 0, everything)
        for o in order[:-1]:
            sends[j, o].wait_recv()
            part[...] += spread(j, o, everything)
        if order:
            sends[j, order[-1]].wait_recv()
        for i in range(pieces):
            cols = slice(i * wide, (i + 1) * wide)
            slabs[0, j, i] = (part[:, cols] + spread(j, order[-1], cols)).astype(BF16)
            for d in range(1, n_outer):
                across[d, j, i] = pltpu.make_async_remote_copy(
                    src_ref=slabs.at[0, j, i],
                    dst_ref=slabs.at[2 * d, j, i],
                    send_sem=y_send.at[d, j, i],
                    recv_sem=y_recv.at[d, j, i],
                    device_id=beyond(d),
                    device_id_type=MESH,
                )
                across[d, j, i].start()
            beside[j, i] = pltpu.make_async_remote_copy(
                src_ref=slabs.at[0, j, i],
                dst_ref=slabs.at[1, j, i],
                send_sem=s_send.at[j, i],
                recv_sem=s_recv.at[j, i],
                device_id=sibling,
                device_id_type=MESH,
            )
            beside[j, i].start()

    def forward(d, j, i):
        across[d, j, i].wait_recv()
        onward[d, j, i] = pltpu.make_async_remote_copy(
            src_ref=slabs.at[2 * d, j, i],
            dst_ref=slabs.at[2 * d + 1, j, i],
            send_sem=f_send.at[d, j, i],
            recv_sem=f_recv.at[d, j, i],
            device_id=sibling,
            device_id_type=MESH,
        )
        onward[d, j, i].start()

    def product(d, i, theirs):
        index = ((outer - d + n_outer) % n_outer) * 2
        index = index + (1 - inner if theirs else inner)
        start = pl.multiple_of(index * slab + i * wide, wide)
        left = jnp.concatenate([slabs[2 * d + theirs, j, i] for j in range(parts)], axis=0)
        return jnp.dot(left, v_ref[pl.ds(start, wide), :], preferred_element_type=F32)

    for j in range(parts):
        if j + 1 < parts:
            for o in order:
                sends[j, o].wait_send()
                sends[j + 1, o].start()
        gather(j)
    load_v.wait()
    for j in range(parts - 1):
        for d in range(1, n_outer):
            for i in range(pieces):
                forward(d, j, i)
    acc[...] = product(0, 0, 0)
    for i in range(1, pieces):
        acc[...] += product(0, i, 0)
    for i in range(pieces):
        for j in range(parts):
            beside[j, i].wait_recv()
        acc[...] += product(0, i, 1)
    for d in range(1, n_outer):
        for i in range(pieces + 1):
            if i < pieces:
                forward(d, parts - 1, i)
                acc[...] += product(d, i, 0)
            if i:
                for j in range(parts):
                    onward[d, j, i - 1].wait_recv()
                acc[...] += product(d, i - 1, 1)

    load_hole.wait()
    live = lax.broadcasted_iota(jnp.int32, (1, acc.shape[0]), 1) < hole_ref[0]
    out_ref[0] = jnp.where(live, acc[...].T, 0.0).astype(BF16)

    for o in order:
        sends[parts - 1, o].wait_send()
    for copies in (across, beside, onward):
        for copy in copies.values():
            copy.wait_send()


def on_device(n_chan, n_kred, t2_ph, dest_owner, source_owner, source_slot, hole_count, ladder_v):
    slab, width = t2_ph.shape[1:]
    capacity = 2 * slab // n_chan
    capacity = -(-capacity // 16) * 16
    total = ladder_v.shape[1]
    wide = 256 if slab % 256 == 0 else slab
    pieces = slab // wide
    n_outer = n_kred // 2
    parts = 2
    tall = width // parts
    dma = pltpu.SemaphoreType.DMA
    return pl.pallas_call(
        functools.partial(kernel, n_chan, n_kred),
        out_shape=pltpu.VMEM((1, slab, width), BF16),
        in_specs=[pl.BlockSpec(memory_space=pltpu.HBM)] * 6,
        out_specs=pl.BlockSpec(memory_space=pltpu.VMEM),
        scratch_shapes=[
            pltpu.VMEM((slab, width), BF16),
            pltpu.VMEM((1, slab), jnp.int32),
            pltpu.VMEM((2, 1, slab), jnp.int32),
            pltpu.SMEM((1,), jnp.int32),
            pltpu.VMEM((n_chan, parts, tall, capacity), BF16),
            pltpu.VMEM((n_chan, parts, tall, capacity), BF16),
            pltpu.VMEM((n_chan, capacity, slab), BF16),
            pltpu.VMEM((n_kred, parts, pieces, tall, wide), BF16),
            pltpu.VMEM((total, slab), BF16),
            pltpu.VMEM((width, slab), F32),
            pltpu.VMEM((tall, slab), F32),
            dma((5,)),
            dma,
            dma((parts, n_chan)),
            dma((parts, n_chan)),
            dma((n_outer, parts, pieces)),
            dma((n_outer, parts, pieces)),
            dma((parts, pieces)),
            dma((parts, pieces)),
            dma((n_outer, parts, pieces)),
            dma((n_outer, parts, pieces)),
        ],
        compiler_params=pltpu.CompilerParams(
            collective_id=0, has_side_effects=True, vmem_limit_bytes=56 * 2**20
        ),
        cost_estimate=pl.CostEstimate(
            flops=2 * total * slab * width, bytes_accessed=2 * total * slab, transcendentals=0
        ),
    )(t2_ph, dest_owner, source_owner, source_slot, hole_count, ladder_v)


def solution(mesh):
    placed = (
        P("chan", "kred", None),
        P("chan", "kred"),
        P("chan", "kred"),
        P("chan", "kred"),
        P("chan"),
        P("chan", None, "kred"),
    )
    return jax.shard_map(
        functools.partial(on_device, mesh.shape["chan"], mesh.shape["kred"]),
        mesh=mesh,
        in_specs=placed,
        out_specs=P("chan", "kred", None),
        check_vma=False,
    )
```

```python
import functools

import jax
import jax.numpy as jnp
from jax import lax
from jax.experimental import pallas as pl
from jax.experimental.pallas import tpu as pltpu
from jax.sharding import PartitionSpec as P

MESH = pl.DeviceIdType.MESH
F32 = jnp.float32
BF16 = jnp.bfloat16


def one_hot(count, row):
    lanes = row.shape[1]
    index = lax.broadcasted_iota(jnp.int32, (count, lanes), 0)
    if count <= 256:
        hit = index.astype(F32).astype(BF16) == row.astype(F32).astype(BF16)
    else:
        hit = index == row
    return jnp.where(hit, jnp.ones((), BF16), jnp.zeros((), BF16))


def row_numbers(owners, n_chan):
    rows = owners.shape[1]
    blocks = rows // 128
    channel = lax.broadcasted_iota(jnp.int32, (n_chan, 128), 0)
    hits = [
        (owners[:, b * 128 : (b + 1) * 128] == channel).astype(F32) for b in range(blocks)
    ]
    above = lax.broadcasted_iota(jnp.int32, (128, 128), 0) < lax.broadcasted_iota(
        jnp.int32, (128, 128), 1
    )
    inside = jnp.dot(
        jnp.concatenate(hits, axis=0).astype(BF16),
        jnp.where(above, 1.0, 0.0).astype(BF16),
        preferred_element_type=F32,
    )
    numbers = []
    offset = jnp.zeros((n_chan, 1), F32)
    for b in range(blocks):
        here = inside[b * n_chan : (b + 1) * n_chan] + offset
        numbers.append(jnp.sum(here * hits[b], axis=0, keepdims=True))
        offset = offset + jnp.sum(hits[b], axis=1, keepdims=True)
    return jnp.concatenate(numbers, axis=1).astype(jnp.int32)


def partners(me, n_chan):
    if n_chan & (n_chan - 1) == 0:

        def flipped(step):
            index, bit = 0, 1
            while bit < n_chan:
                index = index + ((me // bit + step // bit) % 2) * bit
                bit *= 2
            return index

        far = list(range(n_chan // 2, n_chan))
        near = list(range(1, n_chan // 2))
        return flipped, flipped, near, far
    return (
        lambda step: (me + step) % n_chan,
        lambda step: (me - step + n_chan) % n_chan,
        list(range(1, n_chan)),
        [],
    )


def kernel(
    n_chan,
    n_kred,
    cuts,
    t2_hbm,
    dest_hbm,
    owner_hbm,
    slot_hbm,
    hole_vmem,
    v_hbm,
    out_ref,
    t2_ref,
    dest_ref,
    lists,
    outbox,
    arrived,
    picks,
    slabs,
    v_ref,
    acc,
    part,
    in_sem,
    v_sem,
    a_send,
    a_recv,
    y_send,
    y_recv,
    s_send,
    s_recv,
    f_send,
    f_recv,
):
    chan = lax.axis_index("chan")
    kred = lax.axis_index("kred")
    n_outer = n_kred // 2
    inner = kred % 2
    outer = kred // 2
    sibling = {"kred": outer * 2 + (1 - inner)}
    width, capacity = outbox.shape[1:]
    parts = len(cuts) - 1
    bands = [pl.ds(cuts[j], cuts[j + 1] - cuts[j]) for j in range(parts)]
    slab = t2_ref.shape[0]
    pieces, wide = slabs.shape[1], slabs.shape[3]
    receiver, sender, near, far = partners(chan, n_chan)
    order = near + far

    def beyond(d):
        return {"kred": ((outer + d) % n_outer) * 2 + inner}

    load_dest = pltpu.make_async_copy(dest_hbm, dest_ref, in_sem.at[0])
    load_t2 = pltpu.make_async_copy(t2_hbm.at[0], t2_ref, in_sem.at[1])
    load_owner = pltpu.make_async_copy(owner_hbm, lists.at[0], in_sem.at[2])
    load_slot = pltpu.make_async_copy(slot_hbm, lists.at[1], in_sem.at[3])
    load_v = pltpu.make_async_copy(v_hbm.at[0], v_ref, v_sem)
    load_dest.start()
    load_t2.start()
    load_owner.start()
    load_slot.start()

    barrier = pltpu.get_barrier_semaphore()
    for o in order:
        pl.semaphore_signal(
            barrier, inc=1, device_id={"chan": receiver(o)}, device_id_type=MESH
        )
    pl.semaphore_signal(barrier, inc=1, device_id=sibling, device_id_type=MESH)
    for d in range(1, n_outer):
        pl.semaphore_signal(barrier, inc=1, device_id=beyond(d), device_id_type=MESH)

    load_dest.wait()
    owners = dest_ref[...]
    numbers = row_numbers(owners, n_chan)
    load_t2.wait()
    rows = t2_ref[...]

    def pack(target, o, channel):
        choose = one_hot(capacity, jnp.where(owners == channel, numbers, -1))
        target[o] = jnp.dot(choose, rows, preferred_element_type=F32).T.astype(BF16)

    sends = {}
    for at, o in enumerate(far + near):
        pack(outbox, o, receiver(o))
        if at == 0:
            pl.semaphore_wait(barrier, n_chan - 1 + 1 + n_outer - 1)
        for j in range(parts):
            sends[j, o] = pltpu.make_async_remote_copy(
                src_ref=outbox.at[o, bands[j]],
                dst_ref=arrived.at[o, bands[j]],
                send_sem=a_send.at[j, o],
                recv_sem=a_recv.at[j, o],
                device_id={"chan": receiver(o)},
                device_id_type=MESH,
            )
        sends[0, o].start()
    load_v.start()
    pack(arrived, 0, chan)
    load_owner.wait()
    load_slot.wait()
    for o in [0] + order:
        picks[o] = one_hot(capacity, jnp.where(lists[0] == sender(o), lists[1], -1))

    def spread(j, o, cols):
        return jnp.dot(arrived[o, bands[j]], picks[o, :, cols], preferred_element_type=F32)

    across, beside, onward = {}, {}, {}

    def gather(j):
        everything = slice(0, slab)
        some = pl.ds(0, cuts[j + 1] - cuts[j])
        part[some] = spread(j, 0, everything)
        for o in order[:-1]:
            sends[j, o].wait_recv()
            part[some] += spread(j, o, everything)
        if order:
            sends[j, order[-1]].wait_recv()
        for i in range(pieces):
            cols = slice(i * wide, (i + 1) * wide)
            slabs[0, i, bands[j]] = (part[some, cols] + spread(j, order[-1], cols)).astype(BF16)
            for d in range(1, n_outer):
                across[d, j, i] = pltpu.make_async_remote_copy(
                    src_ref=slabs.at[0, i, bands[j]],
                    dst_ref=slabs.at[2 * d, i, bands[j]],
                    send_sem=y_send.at[d, j, i],
                    recv_sem=y_recv.at[d, j, i],
                    device_id=beyond(d),
                    device_id_type=MESH,
                )
                across[d, j, i].start()
            beside[j, i] = pltpu.make_async_remote_copy(
                src_ref=slabs.at[0, i, bands[j]],
                dst_ref=slabs.at[1, i, bands[j]],
                send_sem=s_send.at[j, i],
                recv_sem=s_recv.at[j, i],
                device_id=sibling,
                device_id_type=MESH,
            )
            beside[j, i].start()

    def forward(d, j, i):
        across[d, j, i].wait_recv()
        onward[d, j, i] = pltpu.make_async_remote_copy(
            src_ref=slabs.at[2 * d, i, bands[j]],
            dst_ref=slabs.at[2 * d + 1, i, bands[j]],
            send_sem=f_send.at[d, j, i],
            recv_sem=f_recv.at[d, j, i],
            device_id=sibling,
            device_id_type=MESH,
        )
        onward[d, j, i].start()

    def product(d, i, theirs):
        index = ((outer - d + n_outer) % n_outer) * 2
        index = index + (1 - inner if theirs else inner)
        start = pl.multiple_of(index * slab + i * wide, wide)
        left = slabs[2 * d + theirs, i]
        return jnp.dot(left, v_ref[pl.ds(start, wide), :], preferred_element_type=F32)

    for j in range(parts):
        if j + 1 < parts:
            for o in order:
                sends[j, o].wait_send()
                sends[j + 1, o].start()
        gather(j)
    load_v.wait()
    for j in range(parts - 1):
        for d in range(1, n_outer):
            for i in range(pieces):
                forward(d, j, i)
    acc[...] = product(0, 0, 0)
    for i in range(1, pieces):
        acc[...] += product(0, i, 0)
    for i in range(pieces):
        for j in range(parts):
            beside[j, i].wait_recv()
        acc[...] += product(0, i, 1)
    for d in range(1, n_outer):
        for i in range(pieces + 1):
            if i < pieces:
                forward(d, parts - 1, i)
                acc[...] += product(d, i, 0)
            if i:
                for j in range(parts):
                    onward[d, j, i - 1].wait_recv()
                acc[...] += product(d, i - 1, 1)

    live = lax.broadcasted_iota(jnp.int32, (1, acc.shape[0]), 1) < hole_vmem[...]
    out_ref[0] = jnp.where(live, acc[...].T, 0.0).astype(BF16)

    for o in order:
        sends[parts - 1, o].wait_send()
    for copies in (across, beside, onward):
        for copy in copies.values():
            copy.wait_send()


def on_device(n_chan, n_kred, t2_ph, dest_owner, source_owner, source_slot, hole_count, ladder_v):
    slab, width = t2_ph.shape[1:]
    capacity = 2 * slab // n_chan
    capacity = -(-capacity // 16) * 16
    total = ladder_v.shape[1]
    wide = 256 if slab % 256 == 0 else slab
    pieces = slab // wide
    n_outer = n_kred // 2
    cuts = (0, -(-width * 5 // 128) * 16, width)
    parts = len(cuts) - 1
    dma = pltpu.SemaphoreType.DMA
    return pl.pallas_call(
        functools.partial(kernel, n_chan, n_kred, cuts),
        out_shape=pltpu.VMEM((1, slab, width), BF16),
        in_specs=[pl.BlockSpec(memory_space=pltpu.HBM)] * 4
        + [pl.BlockSpec(memory_space=pltpu.VMEM), pl.BlockSpec(memory_space=pltpu.HBM)],
        out_specs=pl.BlockSpec(memory_space=pltpu.VMEM),
        scratch_shapes=[
            pltpu.VMEM((slab, width), BF16),
            pltpu.VMEM((1, slab), jnp.int32),
            pltpu.VMEM((2, 1, slab), jnp.int32),
            pltpu.VMEM((n_chan, width, capacity), BF16),
            pltpu.VMEM((n_chan, width, capacity), BF16),
            pltpu.VMEM((n_chan, capacity, slab), BF16),
            pltpu.VMEM((n_kred, pieces, width, wide), BF16),
            pltpu.VMEM((total, slab), BF16),
            pltpu.VMEM((width, slab), F32),
            pltpu.VMEM((width, slab), F32),
            dma((4,)),
            dma,
            dma((parts, n_chan)),
            dma((parts, n_chan)),
            dma((n_outer, parts, pieces)),
            dma((n_outer, parts, pieces)),
            dma((parts, pieces)),
            dma((parts, pieces)),
            dma((n_outer, parts, pieces)),
            dma((n_outer, parts, pieces)),
        ],
        compiler_params=pltpu.CompilerParams(
            collective_id=0, has_side_effects=True, vmem_limit_bytes=56 * 2**20
        ),
        cost_estimate=pl.CostEstimate(
            flops=2 * total * slab * width, bytes_accessed=2 * total * slab, transcendentals=0
        ),
    )(t2_ph, dest_owner, source_owner, source_slot, hole_count[:, None], ladder_v)


def solution(mesh):
    placed = (
        P("chan", "kred", None),
        P("chan", "kred"),
        P("chan", "kred"),
        P("chan", "kred"),
        P("chan"),
        P("chan", None, "kred"),
    )
    return jax.shard_map(
        functools.partial(on_device, mesh.shape["chan"], mesh.shape["kred"]),
        mesh=mesh,
        in_specs=placed,
        out_specs=P("chan", "kred", None),
        check_vma=False,
    )
```
